32 devices in a mesh: date: 8 (over y, x, core), az: 4 (over z).
Axes of the slice: x: 2, y: 2, z: 4, core: 2. Of those that a mesh axis runs over, the one named last changes fastest.
Arguments:
- slc: bfloat16 [16, 2, 256, 3072], P('date', None, 'az'), may hold values from -12 to 12
- az_shift: int32 [16], P('date'), may hold values from -4 to 4, as said below
- rg_shift: int32 [16], P('date'), may hold values from -4 to 4, as said below
- az_frac: int32 [16], P('date'), may hold values from 0 to 15
- rg_frac: int32 [16], P('date'), may hold values from 0 to 15
Outputs:
- coherence: bfloat16 [192, 64, 2, 16], P('date', 'az')
- mean_coherence: float32 [192, 64], P('date', 'az')
The draws below stay inside these ranges and needn't reach their ends.
Inputs may be any that keep to these rules, and one draw needn't show every extreme that they name: `az_shift`: date 0 has offset 0; some date has offset 4 and some -4. `rg_shift`: date 0 has offset 0; some date has offset 4 and some -4.
All inputs are finite; a program needn't handle non-finite values.
Results may differ from the reference program's by a relative error of at most 0.0035.
Values may be sent and summed in bfloat16 or wider, within the bound.
A program may use at most 64 MiB of HBM per device.

```python
import math
import jax
import jax.numpy as jnp
from jax import lax

COLS = 3072
TAPS = 8
KBANK = 16
MAXOFF = 4
LOOK_AZ = 4
LOOK_RG = 16
WINDOW = 7
DATES = 16
ROWS = 256


def shift_table(key, which_axis):
    base_key = jax.random.fold_in(key, 7001 + which_axis)
    drawn = jax.random.randint(base_key, (DATES,), -MAXOFF, MAXOFF + 1, dtype=jnp.int32)
    ordering = jax.random.permutation(jax.random.fold_in(base_key, 3), DATES - 1) + 1
    drawn = drawn.at[0].set(0)
    drawn = drawn.at[ordering[0]].set(MAXOFF)
    drawn = drawn.at[ordering[1]].set(-MAXOFF)
    return drawn.astype(jnp.int32)


def draw_az_shift(key, part):
    return shift_table(key, 0)


def draw_rg_shift(key, part):
    return shift_table(key, 1)


def draw_slc(key, part):
    az_table = shift_table(key, 0)
    rg_table = shift_table(key, 1)
    scene_key = jax.random.fold_in(key, 9001)
    extent = (2, ROWS + 2 * MAXOFF, COLS + 2 * MAXOFF)
    scene = jax.random.truncated_normal(jax.random.fold_in(scene_key, 1), -4.0, 4.0, extent, jnp.float32)
    strength = jax.random.uniform(jax.random.fold_in(scene_key, 2), (DATES,), jnp.float32, 0.3, 1.0).at[0].set(1.0)
    phases = jax.random.uniform(jax.random.fold_in(scene_key, 3), (DATES,), jnp.float32, -math.pi, math.pi).at[0].set(0.0)
    noise_key = jax.random.fold_in(scene_key, 4)

    def one_date(date_pos):
        shifted = lax.dynamic_slice(scene, (jnp.int32(0), (MAXOFF - az_table[date_pos]).astype(jnp.int32), (MAXOFF - rg_table[date_pos]).astype(jnp.int32)), (2, ROWS, COLS))
        cosine = jnp.cos(phases[date_pos])
        sine = jnp.sin(phases[date_pos])
        rotated = jnp.stack([shifted[0] * cosine - shifted[1] * sine, shifted[0] * sine + shifted[1] * cosine])
        noise = jax.random.truncated_normal(jax.random.fold_in(noise_key, date_pos), -4.0, 4.0, (2, ROWS, COLS), jnp.float32)
        weight = strength[date_pos]
        mixed = weight * rotated + jnp.sqrt(1.0 - weight * weight) * noise
        return mixed.astype(jnp.bfloat16)
    return lax.map(one_date, jnp.arange(DATES, dtype=jnp.int32))


def place_ends(values, own_key, least, top_value):
    shape = values.shape
    place = [jax.random.randint(jax.random.fold_in(own_key, axis), (), 0, shape[axis]) for axis in range(len(shape))]
    values = values.at[tuple(place)].set(least)
    longest = shape.index(max(shape))
    place[longest] = (place[longest] + 1) % shape[longest]
    return values.at[tuple(place)].set(top_value)


def setup_inputs(seed: int = 0) -> dict:
    seeds = jax.random.split(jax.random.key(seed), 6)
    return {
        "slc": draw_slc(jax.random.fold_in(seeds[5], 71), 0),
        "az_shift": draw_az_shift(jax.random.fold_in(seeds[5], 71), 0),
        "rg_shift": draw_rg_shift(jax.random.fold_in(seeds[5], 71), 0),
        "az_frac": place_ends(jax.random.randint(seeds[3], (DATES,), 0, KBANK), jax.random.fold_in(seeds[3], 1), 0, KBANK - 1).astype(jnp.int32),
        "rg_frac": place_ends(jax.random.randint(seeds[4], (DATES,), 0, KBANK), jax.random.fold_in(seeds[4], 1), 0, KBANK - 1).astype(jnp.int32),
    }


EPS = 1e-06

def kernel_bank():
    fraction = jnp.arange(KBANK, dtype=jnp.float32)[:, None] / KBANK
    tap_place = jnp.arange(TAPS, dtype=jnp.float32)[None, :]
    offset = tap_place - (TAPS // 2 - 1) - fraction
    shaped = jnp.sinc(offset) * (0.5 + 0.5 * jnp.cos(jnp.pi * offset / (TAPS // 2 + 0.5)))
    return shaped / lax.optimization_barrier(jnp.sum(shaped, axis=1, keepdims=True))

def looks_of(values):
    lead = values.shape[:-2]
    rows_in, cols_in = (values.shape[-2], values.shape[-1])
    boxed = values.reshape(lead + (rows_in // LOOK_AZ, LOOK_AZ, cols_in // LOOK_RG, LOOK_RG))
    return lax.optimization_barrier(jnp.mean(boxed, axis=(-3, -1)))

def window_sum(padded):
    radius = WINDOW // 2
    rows_out = padded.shape[-2] - 2 * radius
    cols_out = padded.shape[-1] - 2 * radius
    across = padded[..., 0:rows_out, :]
    for offset_row in range(1, WINDOW):
        across = across + padded[..., offset_row:offset_row + rows_out, :]
    total = across[..., 0:cols_out]
    for offset_col in range(1, WINDOW):
        total = total + across[..., offset_col:offset_col + cols_out]
    return total

def reference(slc, az_shift, rg_shift, az_frac, rg_frac):
    bank = kernel_bank()
    margin = MAXOFF + TAPS // 2
    center = slc[0].astype(jnp.float32)
    power_ref = looks_of(center[0] * center[0] + center[1] * center[1])

    def one_date(packed):
        image, az_offset, rg_offset, az_weights, rg_weights = packed
        padded = jnp.pad(image, ((0, 0), (margin, margin), (margin, margin)))
        ranged = jnp.zeros((2, ROWS + 2 * margin, COLS), jnp.float32)
        for tap_place in range(TAPS):
            start = (margin + rg_offset + tap_place - (TAPS // 2 - 1)).astype(jnp.int32)
            ranged = ranged + rg_weights[tap_place] * lax.dynamic_slice_in_dim(padded, start, COLS, 2).astype(jnp.float32)
        resampled = jnp.zeros((2, ROWS, COLS), jnp.float32)
        for tap_place in range(TAPS):
            start = (margin + az_offset + tap_place - (TAPS // 2 - 1)).astype(jnp.int32)
            resampled = resampled + az_weights[tap_place] * lax.dynamic_slice_in_dim(ranged, start, ROWS, 1)
        real_part = center[0] * resampled[0] + center[1] * resampled[1]
        imag_part = center[1] * resampled[0] - center[0] * resampled[1]
        power_sec = resampled[0] * resampled[0] + resampled[1] * resampled[1]
        return looks_of(jnp.stack([real_part, imag_part, power_sec]))
    looks = lax.map(one_date, (slc, az_shift, rg_shift, bank[az_frac], bank[rg_frac]))
    radius = WINDOW // 2
    summed = window_sum(jnp.pad(looks, ((0, 0), (0, 0), (radius, radius), (radius, radius))))
    summed_ref = window_sum(jnp.pad(power_ref, ((radius, radius), (radius, radius))))
    scale = 1.0 / jnp.sqrt(summed_ref[None] * summed[:, 2] + EPS)
    gamma = jnp.stack([summed[:, 0] * scale, summed[:, 1] * scale], axis=1).astype(jnp.bfloat16)
    gamma = lax.optimization_barrier(gamma)
    as_float = gamma.astype(jnp.float32)
    magnitude = jnp.sqrt(as_float[:, 0] * as_float[:, 0] + as_float[:, 1] * as_float[:, 1])
    average = lax.optimization_barrier(jnp.mean(magnitude, axis=0))
    return (jnp.transpose(gamma, (3, 2, 1, 0)), jnp.transpose(average, (1, 0)))
```

```python
import functools

import jax
import jax.numpy as jnp
import numpy as np
from jax import lax
from jax.experimental import pallas as pl
from jax.experimental.pallas import tpu as pltpu
from jax.sharding import PartitionSpec as P

TAPS = 8
KBANK = 16
MAXOFF = 4
LOOK_AZ = 4
LOOK_RG = 16
WINDOW = 7
EPS = 1e-06

LEFT = TAPS // 2 - 1
RADIUS = WINDOW // 2
RIM = MAXOFF + TAPS // 2
LANE = 128
BLOCK = 2 * LANE
CHUNK = 16
MESH = pl.DeviceIdType.MESH


def kernel_bank():
    fraction = np.arange(KBANK, dtype=np.float64)[:, None] / KBANK
    offset = np.arange(TAPS, dtype=np.float64)[None, :] - LEFT - fraction
    shaped = np.sinc(offset) * (0.5 + 0.5 * np.cos(np.pi * offset / (TAPS // 2 + 0.5)))
    return (shaped / shaped.sum(axis=1, keepdims=True)).astype(np.float32)


def column_boxes(cols, lanes):
    look = np.arange(cols)[:, None] // LOOK_RG
    place = np.arange(lanes)[None, :]
    inside = (np.abs(look - place) <= RADIUS) & (place < cols // LOOK_RG)
    return jnp.asarray(inside, jnp.bfloat16)


def row_boxes(kinds, rows):
    looks = rows // LOOK_AZ
    kind_in = np.arange(kinds * rows) // rows
    look_in = (np.arange(kinds * rows) % rows) // LOOK_AZ
    kind_out = np.concatenate([np.repeat(np.arange(kinds), looks)] + [np.repeat(np.arange(kinds), 8)] * 2)
    look_out = np.concatenate(
        [
            np.tile(np.arange(looks), kinds),
            np.tile(np.arange(8) - 8, kinds),
            np.tile(np.arange(8) + looks, kinds),
        ]
    )
    inside = (kind_in[None] == kind_out[:, None]) & (np.abs(look_in[None] - look_out[:, None]) <= RADIUS)
    return jnp.asarray(inside / (LOOK_AZ * LOOK_RG), jnp.bfloat16)


def two_terms(x):
    high = x.astype(jnp.bfloat16)
    return high, (x - high.astype(jnp.float32)).astype(jnp.bfloat16)


def banded(tap, weights):
    out = jnp.zeros(tap.shape, jnp.float32)
    for j in range(TAPS):
        out = jnp.where(tap == j, weights[j], out)
    return out


def dot(a, b):
    return jnp.dot(a, b, preferred_element_type=jnp.float32)


def kernel(
    n, n_az, dates, rows, cols,
    az_shift, rg_shift, az_frac, rg_frac, bank, slc, boxes_hbm, row_box,
    coh_ref, mean_ref,
    own, rim_out, rim_in, center, boxes, toep, azm, ranged, sec, prod, looks, edge_out, edge_in,
    strip_out, strip_in,
    load_sem, box_sem, own_sem, rim_send, rim_recv, c_ring, c_core, c_recv, e_send, e_recv, s_send, s_recv,
):
    me, az = lax.axis_index("date"), lax.axis_index("az")
    pair = 2 if n % 2 == 0 and n >= 4 else 1
    chips = n // pair
    chip, core = me // pair, me % pair

    def snake(p):
        return (p // 2) * 2 + (p + p // 2) % 2

    pos = snake(chip)
    onward = snake((pos + 1) % chips) * pair + core
    back = snake((pos + chips - 1) % chips) * pair + core
    up, down = jnp.maximum(az - 1, 0), jnp.minimum(az + 1, n_az - 1)
    has_up, has_down = az > 0, az < n_az - 1

    kinds = 3 * dates + 1
    look_rows = rows // LOOK_AZ
    strip = cols // LOOK_RG // n
    n_blocks = cols // BLOCK
    inner = pl.ds(LANE, cols)

    loads = [
        pltpu.make_async_copy(slc.at[d, c], own.at[d, pl.ds(c * rows, rows), inner], load_sem.at[d, c])
        for d in range(dates)
        for c in range(2)
    ]
    for load in loads:
        load.start()
    box_load = pltpu.make_async_copy(boxes_hbm, boxes, box_sem)
    box_load.start()

    barrier = pltpu.get_barrier_semaphore()

    def greet(s, _):
        pl.semaphore_signal(barrier, inc=1, device_id=((me + s) % n, az), device_id_type=MESH)
        return 0

    lax.fori_loop(1, n, greet, 0)

    @pl.when(has_up)
    def _():
        pl.semaphore_signal(barrier, inc=1, device_id=(me, up), device_id_type=MESH)

    @pl.when(has_down)
    def _():
        pl.semaphore_signal(barrier, inc=1, device_id=(me, down), device_id_type=MESH)

    for d in range(dates):
        for lo in (0, LANE + cols):
            own[d, :, lo : lo + LANE] = jnp.zeros((2 * rows, LANE), jnp.bfloat16)
            for side in range(2):
                rim_in[side, d, :, lo : lo + LANE] = jnp.zeros((2 * RIM, LANE), jnp.bfloat16)

    @pl.when(jnp.logical_not(has_up))
    def _():
        rim_in[0, :, :, LANE : LANE + cols] = jnp.zeros((dates, 2 * RIM, cols), jnp.bfloat16)
        edge_in[0] = jnp.zeros(edge_in.shape[1:], jnp.float32)

    @pl.when(jnp.logical_not(has_down))
    def _():
        rim_in[1, :, :, LANE : LANE + cols] = jnp.zeros((dates, 2 * RIM, cols), jnp.bfloat16)
        edge_in[1] = jnp.zeros(edge_in.shape[1:], jnp.float32)

    for load in loads:
        load.wait()

    for d in range(dates):
        for side, lo in ((0, 0), (1, rows - 16)):
            cut = slice(0, RIM) if side == 0 else slice(16 - RIM, 16)
            both = [
                own[d, c * rows + lo : c * rows + lo + 16, LANE : LANE + cols].astype(jnp.float32)[cut]
                for c in range(2)
            ]
            rim_out[side, d] = jnp.concatenate(both, axis=0).astype(jnp.bfloat16)

    n_here = has_up.astype(jnp.int32) + has_down.astype(jnp.int32)
    pl.semaphore_wait(barrier, n - 1 + n_here)

    def rim_copy(side):
        return pltpu.make_async_remote_copy(
            src_ref=rim_out.at[side],
            dst_ref=rim_in.at[1 - side, :, :, inner],
            send_sem=rim_send.at[side],
            recv_sem=rim_recv.at[1 - side],
            device_id=(me, up if side == 0 else down),
            device_id_type=MESH,
        )

    per_part = rows // CHUNK

    def place(i, part):
        return i % 2, pl.ds(pl.multiple_of((i // 2) * CHUNK + part * (rows // 2), CHUNK), CHUNK)

    def chunk_copy(i, part, source, to, sems):
        c, r = place(i, part)
        return pltpu.make_async_remote_copy(
            src_ref=source.at[c, r, :],
            dst_ref=center.at[c, r, :],
            send_sem=sems.at[part, i],
            recv_sem=c_recv.at[part, i],
            device_id=(to, az),
            device_id_type=MESH,
        )

    is_source = jnp.logical_and(pos == 0, core == 0)
    relay = jnp.logical_and(pos > 0, core == 0)
    sibling = chip * pair + 1
    own_center = pltpu.make_async_copy(slc.at[0], center, own_sem)

    @pl.when(is_source)
    def _():
        for i in range(per_part):
            for part, to in ((0, onward), (1, back)):
                chunk_copy(i, part, slc.at[0], to, c_ring).start()
        for i in range(per_part):
            for part in range(2):
                if pair == 2:
                    chunk_copy(i, part, slc.at[0], sibling, c_core).start()
        own_center.start()

    @pl.when(has_up)
    def _():
        rim_copy(0).start()

    @pl.when(has_down)
    def _():
        rim_copy(1).start()

    def relay_step(t):
        for part, i, last, to in ((0, t - pos, chips - 1, onward), (1, t - (chips - pos), 1, back)):

            @pl.when(relay & (i >= 0) & (i < per_part))
            def _():
                chunk_copy(i, part, center, to, c_ring).wait_recv()

                @pl.when(pos != last)
                def _():
                    chunk_copy(i, part, center, to, c_ring).start()

                if pair == 2:
                    chunk_copy(i, part, center, sibling, c_core).start()

    steps = [functools.partial(relay_step, t) for t in range(1, chips + per_part - 1)]

    for d in range(dates):
        weights = [bank[rg_frac[d], j] for j in range(TAPS)]
        across = lax.broadcasted_iota(jnp.int32, (LANE, LANE), 0) - lax.broadcasted_iota(jnp.int32, (LANE, LANE), 1)
        for b in range(3):
            terms = two_terms(banded(across + (LANE * (b - 1) + LEFT - rg_shift[d]), weights))
            for k in range(2):
                for right in range(2):
                    toep[d, k, LANE * (b + right) : LANE * (b + right + 1), LANE * right : LANE * (right + 1)] = terms[k]
        for k in range(2):
            zero = jnp.zeros((LANE, LANE), jnp.bfloat16)
            toep[d, k, 0:LANE, LANE:] = zero
            toep[d, k, 3 * LANE :, 0:LANE] = zero

    deep = 2 * rows + 4 * RIM
    for d in range(dates):
        weights = [bank[az_frac[d], j] for j in range(TAPS)]
        out = lax.broadcasted_iota(jnp.int32, (2 * rows, deep), 0)
        src = lax.broadcasted_iota(jnp.int32, (2 * rows, deep), 1)
        rim = src - 2 * rows
        in_own = rim < 0
        rim = jnp.maximum(rim, 0)
        rim_row = lax.rem(rim, RIM)
        src_part = jnp.where(in_own, lax.div(src, rows), lax.rem(lax.div(rim, RIM), 2))
        src_row = jnp.where(in_own, lax.rem(src, rows), jnp.where(rim < 2 * RIM, rim_row - RIM, rim_row + rows))
        tap = src_row - lax.rem(out, rows) + (LEFT - az_shift[d])
        tap = jnp.where(src_part == lax.div(out, rows), tap, -1)
        terms = two_terms(banded(tap, weights))
        for k in range(2):
            azm[d, k * 2 * rows : (k + 1) * 2 * rows, :] = terms[k]

    def range_block(k, _):
        window = pl.ds(pl.multiple_of(k * BLOCK, LANE), 2 * BLOCK)
        here = pl.ds(pl.multiple_of(k * BLOCK, LANE), BLOCK)
        for d in range(dates):
            x = own[d, :, window]
            ranged[d, 0 : 2 * rows, here] = (dot(x, toep[d, 0]) + dot(x, toep[d, 1])).astype(jnp.bfloat16)
        return 0

    done = 0
    for t, step in enumerate(steps):
        step()
        until = min(n_blocks, -(-n_blocks * (t + 1) // min(len(steps), 4)))
        if until > done:
            lax.fori_loop(done, until, range_block, 0)
            done = until

    @pl.when(has_up)
    def _():
        rim_copy(1).wait_recv()

    @pl.when(has_down)
    def _():
        rim_copy(0).wait_recv()

    def az_block(k, _):
        window = pl.ds(pl.multiple_of(k * BLOCK, LANE), 2 * BLOCK)
        here = pl.ds(pl.multiple_of(k * BLOCK, LANE), BLOCK)
        for d in range(dates):
            x = jnp.concatenate([rim_in[0, d, :, window], rim_in[1, d, :, window]], axis=0)
            ranged[d, 2 * rows :, here] = (dot(x, toep[d, 0]) + dot(x, toep[d, 1])).astype(jnp.bfloat16)
            both = dot(azm[d], ranged[d, :, here])
            s = both[0 : 2 * rows] + both[2 * rows :]
            sec[d, :, here] = s.astype(jnp.bfloat16)
            power = s[0:rows] * s[0:rows] + s[rows:] * s[rows:]
            prod[(3 * d + 2) * rows : (3 * d + 3) * rows, here] = power.astype(jnp.bfloat16)
        return 0

    lax.fori_loop(0, n_blocks, az_block, 0)

    @pl.when(is_source)
    def _():
        own_center.wait()

    @pl.when(core != 0)
    def _():
        for i in range(per_part):
            for part in range(2):
                chunk_copy(i, part, center, onward, c_ring).wait_recv()

    def cross_block(k, _):
        here = pl.ds(pl.multiple_of(k * BLOCK, LANE), BLOCK)
        e0, e1 = center[0, :, here].astype(jnp.float32), center[1, :, here].astype(jnp.float32)
        for d in range(dates):
            s0 = sec[d, 0:rows, here].astype(jnp.float32)
            s1 = sec[d, rows:, here].astype(jnp.float32)
            prod[3 * d * rows : (3 * d + 1) * rows, here] = (e0 * s0 + e1 * s1).astype(jnp.bfloat16)
            prod[(3 * d + 1) * rows : (3 * d + 2) * rows, here] = (e1 * s0 - e0 * s1).astype(jnp.bfloat16)
        prod[3 * dates * rows :, here] = (e0 * e0 + e1 * e1).astype(jnp.bfloat16)
        return 0

    lax.fori_loop(0, n_blocks, cross_block, 0)

    box_load.wait()
    high, low = two_terms(dot(prod[...], boxes[...]))
    looks[...] = dot(row_box[...], high) + dot(row_box[...], low)
    n_own = kinds * look_rows
    edge_out[0] = looks[n_own : n_own + 8 * kinds, :]
    edge_out[1] = looks[n_own + 8 * kinds :, :]

    def edge_copy(side):
        return pltpu.make_async_remote_copy(
            src_ref=edge_out.at[side],
            dst_ref=edge_in.at[1 - side],
            send_sem=e_send.at[side],
            recv_sem=e_recv.at[1 - side],
            device_id=(me, up if side == 0 else down),
            device_id_type=MESH,
        )

    @pl.when(has_up)
    def _():
        edge_copy(0).start()

    @pl.when(has_down)
    def _():
        edge_copy(1).start()

    @pl.when(has_up)
    def _():
        edge_copy(1).wait_recv()

    @pl.when(has_down)
    def _():
        edge_copy(0).wait_recv()

    def summed(kind):
        here = looks[kind * look_rows : (kind + 1) * look_rows, :]
        above = edge_in[0, 8 * kind : 8 * kind + 8, :]
        below = edge_in[1, 8 * kind : 8 * kind + 8, :]
        parts = [here[0:8] + above, here[look_rows - 8 :] + below]
        if look_rows > 16:
            parts.insert(1, here[8 : look_rows - 8])
        return jnp.concatenate(parts, axis=0)

    reference_power = summed(3 * dates)
    parts = [[], []]
    for d in range(dates):
        scale = 1.0 / jnp.sqrt(reference_power * summed(3 * d + 2) + EPS)
        for c in range(2):
            parts[c].append(summed(3 * d + c) * scale)
    gamma = jnp.concatenate(parts[0] + parts[1], axis=0)
    gamma = gamma.astype(jnp.bfloat16).astype(jnp.float32)
    used = 2 * dates * look_rows
    if used < LANE:
        gamma = jnp.concatenate([gamma, jnp.zeros((LANE - used, gamma.shape[1]), jnp.float32)], axis=0)
    turned = gamma.T
    for j in range(n):
        strip_out[j] = turned[j * strip : (j + 1) * strip, :]

    def strip_copy(to, slot):
        return pltpu.make_async_remote_copy(
            src_ref=strip_out.at[to],
            dst_ref=strip_in.at[slot],
            send_sem=s_send.at[to],
            recv_sem=s_recv.at[slot],
            device_id=(to, az),
            device_id_type=MESH,
        )

    def send_strip(s, _):
        strip_copy((me + s) % n, me).start()
        return 0

    lax.fori_loop(1, n, send_strip, 0)
    strip_in[me] = strip_out[me]

    @pl.when(has_up)
    def _():
        rim_copy(0).wait_send()
        edge_copy(0).wait_send()

    @pl.when(has_down)
    def _():
        rim_copy(1).wait_send()
        edge_copy(1).wait_send()

    for part, last, to in ((0, chips - 1, onward), (1, 1, back)):

        @pl.when((core == 0) & (pos != last))
        def _():
            for i in range(per_part):
                chunk_copy(i, part, center, to, c_ring).wait_send()

        if pair == 2:

            @pl.when(core == 0)
            def _():
                for i in range(per_part):
                    chunk_copy(i, part, center, sibling, c_core).wait_send()

    def hear_strip(s, _):
        other = (me + s) % n
        strip_copy(other, other).wait_recv()
        strip_copy(other, other).wait_send()
        return 0

    lax.fori_loop(1, n, hear_strip, 0)

    half = dates * look_rows
    coh_ref[...] = strip_in[...]

    def magnitude(j, total):
        v = strip_in[j]
        sq = v * v
        return total + jnp.sqrt(sq[:, 0:half] + sq[:, half : 2 * half])

    total = lax.fori_loop(0, n, magnitude, jnp.zeros((strip, half), jnp.float32))
    mean = total[:, 0:look_rows]
    for d in range(1, dates):
        mean = mean + total[:, d * look_rows : (d + 1) * look_rows]
    mean_ref[...] = mean * (1.0 / (n * dates))


def body(n, n_az, slc, az_shift, rg_shift, az_frac, rg_frac):
    dates, _, rows, cols = slc.shape
    kinds = 3 * dates + 1
    look_rows, look_cols = rows // LOOK_AZ, cols // LOOK_RG
    lanes = -(-look_cols // LANE) * LANE
    strip = look_cols // n
    wide = -(-2 * dates * look_rows // LANE) * LANE
    per_part = rows // CHUNK
    bf, f32 = jnp.bfloat16, jnp.float32
    smem = pl.BlockSpec(memory_space=pltpu.SMEM)
    vmem = pl.BlockSpec(memory_space=pltpu.VMEM)
    anym = pl.BlockSpec(memory_space=pl.ANY)
    dma = pltpu.SemaphoreType.DMA
    strips, mean = pl.pallas_call(
        functools.partial(kernel, n, n_az, dates, rows, cols),
        out_shape=(
            jax.ShapeDtypeStruct((n, strip, wide), f32),
            jax.ShapeDtypeStruct((strip, look_rows), f32),
        ),
        in_specs=[smem] * 5 + [anym, anym, vmem],
        out_specs=(vmem, vmem),
        scratch_shapes=[
            pltpu.VMEM((dates, 2 * rows, cols + 2 * LANE), bf),
            pltpu.VMEM((2, dates, 2 * RIM, cols), bf),
            pltpu.VMEM((2, dates, 2 * RIM, cols + 2 * LANE), bf),
            pltpu.VMEM((2, rows, cols), bf),
            pltpu.VMEM((cols, lanes), bf),
            pltpu.VMEM((dates, 2, 2 * BLOCK, BLOCK), bf),
            pltpu.VMEM((dates, 4 * rows, 2 * rows + 4 * RIM), bf),
            pltpu.VMEM((dates, 2 * rows + 4 * RIM, cols), bf),
            pltpu.VMEM((dates, 2 * rows, cols), bf),
            pltpu.VMEM((kinds * rows, cols), bf),
            pltpu.VMEM((kinds * (look_rows + 16), lanes), f32),
            pltpu.VMEM((2, 8 * kinds, lanes), f32),
            pltpu.VMEM((2, 8 * kinds, lanes), f32),
            pltpu.VMEM((n, strip, wide), f32),
            pltpu.VMEM((n, strip, wide), f32),
            dma((dates, 2)),
            dma,
            dma,
            dma((2,)),
            dma((2,)),
            dma((2, per_part)),
            dma((2, per_part)),
            dma((2, per_part)),
            dma((2,)),
            dma((2,)),
            dma((n,)),
            dma((n,)),
        ],
        compiler_params=pltpu.CompilerParams(
            collective_id=0, has_side_effects=True, vmem_limit_bytes=48 * 1024 * 1024
        ),
    )(
        az_shift, rg_shift, az_frac, rg_frac, jnp.asarray(kernel_bank()), slc,
        column_boxes(cols, lanes), row_boxes(kinds, rows),
    )
    strips = strips[:, :, : 2 * dates * look_rows].reshape(n, strip, 2, dates, look_rows)
    coherence = jnp.transpose(strips, (1, 4, 2, 0, 3)).reshape(strip, look_rows, 2, n * dates)
    return coherence.astype(jnp.bfloat16), mean


def solution(mesh):
    placed = (P("date", None, "az", None), P("date"), P("date"), P("date"), P("date"))
    return jax.shard_map(
        functools.partial(body, mesh.shape["date"], mesh.shape["az"]),
        mesh=mesh,
        in_specs=placed,
        out_specs=(P("date", "az", None, None), P("date", "az")),
        check_vma=False,
    )
```

```python
import functools

import jax
import jax.numpy as jnp
import numpy as np
from jax import lax
from jax.experimental import pallas as pl
from jax.experimental.pallas import tpu as pltpu
from jax.sharding import PartitionSpec as P

TAPS = 8
KBANK = 16
MAXOFF = 4
LOOK_AZ = 4
LOOK_RG = 16
WINDOW = 7
EPS = 1e-06

LEFT = TAPS // 2 - 1
RADIUS = WINDOW // 2
RIM = MAXOFF + TAPS // 2
LANE = 128
BLOCK = 2 * LANE
CHUNK = 16
PIECES = 4
MESH = pl.DeviceIdType.MESH


def kernel_bank():
    fraction = np.arange(KBANK, dtype=np.float64)[:, None] / KBANK
    offset = np.arange(TAPS, dtype=np.float64)[None, :] - LEFT - fraction
    shaped = np.sinc(offset) * (0.5 + 0.5 * np.cos(np.pi * offset / (TAPS // 2 + 0.5)))
    return (shaped / shaped.sum(axis=1, keepdims=True)).astype(np.float32)


def column_boxes(cols, lanes):
    look = np.arange(cols)[:, None] // LOOK_RG
    place = np.arange(lanes)[None, :]
    inside = (np.abs(look - place) <= RADIUS) & (place < cols // LOOK_RG)
    return jnp.asarray(inside, jnp.bfloat16)


def row_boxes(kinds, rows):
    looks = rows // LOOK_AZ
    kind_in = np.arange(kinds * rows) // rows
    look_in = (np.arange(kinds * rows) % rows) // LOOK_AZ
    kind_out = np.concatenate([np.repeat(np.arange(kinds), looks)] + [np.repeat(np.arange(kinds), 8)] * 2)
    look_out = np.concatenate(
        [
            np.tile(np.arange(looks), kinds),
            np.tile(np.arange(8) - 8, kinds),
            np.tile(np.arange(8) + looks, kinds),
        ]
    )
    inside = (kind_in[None] == kind_out[:, None]) & (np.abs(look_in[None] - look_out[:, None]) <= RADIUS)
    return jnp.asarray(inside / (LOOK_AZ * LOOK_RG), jnp.bfloat16)


def two_terms(x):
    high = x.astype(jnp.bfloat16)
    return high, (x - high.astype(jnp.float32)).astype(jnp.bfloat16)


def banded(tap, weights):
    out = jnp.zeros(tap.shape, jnp.float32)
    for j in range(TAPS):
        out = jnp.where(tap == j, weights[j], out)
    return out


def dot(a, b):
    return jnp.dot(a, b, preferred_element_type=jnp.float32)


def kernel(
    n, n_az, dates, rows, cols,
    az_shift, rg_shift, az_frac, rg_frac, bank, slc, boxes_hbm, row_box,
    coh_ref, mean_ref,
    own, rim_out, rim_in, center, boxes, toep, azm, ranged, sec, prod, looks, edge_out, edge_in,
    strip_out, strip_in,
    load_sem, box_sem, own_sem, rim_send, rim_recv, c_ring, c_core, c_recv, e_send, e_recv, s_send, s_recv,
):
    me, az = lax.axis_index("date"), lax.axis_index("az")
    chips = n // 2
    chip, core = me // 2, me % 2
    n_pieces = c_recv.shape[2]
    piece = 2 * cols // n_pieces

    def snake(p):
        return (p // 2) * 2 + (p + p // 2) % 2

    pos = snake(chip)
    onward = snake((pos + 1) % chips) * 2 + core
    back = snake((pos + chips - 1) % chips) * 2 + core
    up, down = jnp.maximum(az - 1, 0), jnp.minimum(az + 1, n_az - 1)
    has_up, has_down = az > 0, az < n_az - 1

    kinds = 3 * dates + 1
    look_rows = rows // LOOK_AZ
    strip = cols // LOOK_RG // n
    n_blocks = cols // BLOCK
    inner = pl.ds(LANE, cols)

    loads = [
        pltpu.make_async_copy(slc.at[d, c], own.at[d, pl.ds(c * rows, rows), inner], load_sem.at[d, c])
        for d in range(dates)
        for c in range(2)
    ]
    for load in loads:
        load.start()
    box_load = pltpu.make_async_copy(boxes_hbm, boxes, box_sem)
    box_load.start()

    barrier = pltpu.get_barrier_semaphore()

    def greet(s, _):
        pl.semaphore_signal(barrier, inc=1, device_id=((me + s) % n, az), device_id_type=MESH)
        return 0

    lax.fori_loop(1, n, greet, 0)

    @pl.when(has_up)
    def _():
        pl.semaphore_signal(barrier, inc=1, device_id=(me, up), device_id_type=MESH)

    @pl.when(has_down)
    def _():
        pl.semaphore_signal(barrier, inc=1, device_id=(me, down), device_id_type=MESH)

    for d in range(dates):
        for lo in (0, LANE + cols):
            own[d, :, lo : lo + LANE] = jnp.zeros((2 * rows, LANE), jnp.bfloat16)
            for side in range(2):
                rim_in[side, d, :, lo : lo + LANE] = jnp.zeros((2 * RIM, LANE), jnp.bfloat16)

    @pl.when(jnp.logical_not(has_up))
    def _():
        rim_in[0, :, :, LANE : LANE + cols] = jnp.zeros((dates, 2 * RIM, cols), jnp.bfloat16)
        edge_in[0] = jnp.zeros(edge_in.shape[1:], jnp.float32)

    @pl.when(jnp.logical_not(has_down))
    def _():
        rim_in[1, :, :, LANE : LANE + cols] = jnp.zeros((dates, 2 * RIM, cols), jnp.bfloat16)
        edge_in[1] = jnp.zeros(edge_in.shape[1:], jnp.float32)

    for load in loads:
        load.wait()

    for d in range(dates):
        for side, lo in ((0, 0), (1, rows - 16)):
            cut = slice(0, RIM) if side == 0 else slice(16 - RIM, 16)
            both = [
                own[d, c * rows + lo : c * rows + lo + 16, LANE : LANE + cols].astype(jnp.float32)[cut]
                for c in range(2)
            ]
            rim_out[side, d] = jnp.concatenate(both, axis=0).astype(jnp.bfloat16)

    n_here = has_up.astype(jnp.int32) + has_down.astype(jnp.int32)
    pl.semaphore_wait(barrier, n - 1 + n_here)

    def rim_copy(side):
        return pltpu.make_async_remote_copy(
            src_ref=rim_out.at[side],
            dst_ref=rim_in.at[1 - side, :, :, inner],
            send_sem=rim_send.at[side],
            recv_sem=rim_recv.at[1 - side],
            device_id=(me, up if side == 0 else down),
            device_id_type=MESH,
        )

    def place(i, way, stream):
        r = pl.multiple_of(way * (rows // 2) + stream * (rows // 4), CHUNK)
        c = pl.multiple_of((i // 2) * piece, LANE)
        return i % 2, pl.ds(r, rows // 4), pl.ds(c, piece)

    def chunk_copy(i, way, stream, source, to, send_sem):
        where = place(i, way, stream)
        return pltpu.make_async_remote_copy(
            src_ref=source.at[where],
            dst_ref=center.at[where],
            send_sem=send_sem,
            recv_sem=c_recv.at[way, stream, i],
            device_id=(to, az),
            device_id_type=MESH,
        )

    def ring_copy(i, way, stream, source):
        return chunk_copy(i, way, stream, source, onward if way == 0 else back, c_ring.at[way, i])

    def core_copy(i, way, stream, source):
        return chunk_copy(i, way, stream, source, sibling, c_core.at[way, stream, i])

    is_source = jnp.logical_and(pos == 0, core == 0)
    sibling = chip * 2 + (1 - core)
    own_center = pltpu.make_async_copy(slc.at[0], center, own_sem)

    @pl.when(is_source)
    def _():
        for i in range(n_pieces):
            for way in range(2):
                core_copy(i, way, 1, slc.at[0]).start()
                ring_copy(i, way, 0, slc.at[0]).start()
        for i in range(n_pieces):
            for way in range(2):
                core_copy(i, way, 0, slc.at[0]).start()
        own_center.start()

    @pl.when(has_up)
    def _():
        rim_copy(0).start()

    @pl.when(has_down)
    def _():
        rim_copy(1).start()

    def relay_step(t):
        for way, hops, last in ((0, pos, chips - 1), (1, (chips - pos) % chips, 1)):
            i = t - hops - core

            @pl.when(jnp.logical_not(is_source) & (i >= 0) & (i < n_pieces))
            def _():
                ring_copy(i, way, core, center).wait_recv()

                @pl.when(pos != last)
                def _():
                    ring_copy(i, way, core, center).start()

                @pl.when(pos > 0)
                def _():
                    core_copy(i, way, core, center).start()

    steps = [functools.partial(relay_step, t) for t in range(1, chips + n_pieces)]

    for d in range(dates):
        weights = [bank[rg_frac[d], j] for j in range(TAPS)]
        across = lax.broadcasted_iota(jnp.int32, (LANE, LANE), 0) - lax.broadcasted_iota(jnp.int32, (LANE, LANE), 1)
        for b in range(3):
            terms = two_terms(banded(across + (LANE * (b - 1) + LEFT - rg_shift[d]), weights))
            for k in range(2):
                for right in range(2):
                    toep[d, k, LANE * (b + right) : LANE * (b + right + 1), LANE * right : LANE * (right + 1)] = terms[k]
        for k in range(2):
            zero = jnp.zeros((LANE, LANE), jnp.bfloat16)
            toep[d, k, 0:LANE, LANE:] = zero
            toep[d, k, 3 * LANE :, 0:LANE] = zero

    deep = 2 * rows + 4 * RIM
    for d in range(dates):
        weights = [bank[az_frac[d], j] for j in range(TAPS)]
        out = lax.broadcasted_iota(jnp.int32, (2 * rows, deep), 0)
        src = lax.broadcasted_iota(jnp.int32, (2 * rows, deep), 1)
        rim = src - 2 * rows
        in_own = rim < 0
        rim = jnp.maximum(rim, 0)
        rim_row = lax.rem(rim, RIM)
        src_part = jnp.where(in_own, lax.div(src, rows), lax.rem(lax.div(rim, RIM), 2))
        src_row = jnp.where(in_own, lax.rem(src, rows), jnp.where(rim < 2 * RIM, rim_row - RIM, rim_row + rows))
        tap = src_row - lax.rem(out, rows) + (LEFT - az_shift[d])
        tap = jnp.where(src_part == lax.div(out, rows), tap, -1)
        terms = two_terms(banded(tap, weights))
        for k in range(2):
            azm[d, k * 2 * rows : (k + 1) * 2 * rows, :] = terms[k]

    def range_block(k, _):
        window = pl.ds(pl.multiple_of(k * BLOCK, LANE), 2 * BLOCK)
        here = pl.ds(pl.multiple_of(k * BLOCK, LANE), BLOCK)
        for d in range(dates):
            x = own[d, :, window]
            ranged[d, 0 : 2 * rows, here] = (dot(x, toep[d, 0]) + dot(x, toep[d, 1])).astype(jnp.bfloat16)
        return 0

    def range_rims(_):
        @pl.when(has_up)
        def _():
            rim_copy(1).wait_recv()

        @pl.when(has_down)
        def _():
            rim_copy(0).wait_recv()

        for d in range(dates):
            x = jnp.concatenate(
                [rim_in[side, d, :, k * BLOCK : (k + 2) * BLOCK] for k in range(n_blocks) for side in range(2)], axis=0
            )
            y = (dot(x, toep[d, 0]) + dot(x, toep[d, 1])).astype(jnp.bfloat16)
            for k in range(n_blocks):
                ranged[d, 2 * rows :, k * BLOCK : (k + 1) * BLOCK] = y[4 * RIM * k : 4 * RIM * (k + 1)]

    def az_block(k, _):
        here = pl.ds(pl.multiple_of(k * BLOCK, LANE), BLOCK)
        for d in range(dates):
            both = dot(azm[d], ranged[d, :, here])
            s = both[0 : 2 * rows] + both[2 * rows :]
            sec[d, :, here] = s.astype(jnp.bfloat16)
            power = s[0:rows] * s[0:rows] + s[rows:] * s[rows:]
            prod[(3 * d + 2) * rows : (3 * d + 3) * rows, here] = power.astype(jnp.bfloat16)
        return 0

    third = n_blocks // 3
    work = [functools.partial(lax.fori_loop, k * third, (k + 1) * third, range_block) for k in range(3)]
    work += [range_rims]
    work += [functools.partial(lax.fori_loop, k * third, (k + 1) * third, az_block) for k in range(3)]
    for k in range(max(len(steps), len(work))):
        if k < len(work):
            work[k](0)
        if k < len(steps):
            steps[k]()

    @pl.when(is_source)
    def _():
        own_center.wait()

    @pl.when(jnp.logical_not(is_source))
    def _():
        for i in range(n_pieces):
            for way in range(2):
                core_copy(i, way, 1 - core, center).wait_recv()

    def cross_block(k, _):
        here = pl.ds(pl.multiple_of(k * BLOCK, LANE), BLOCK)
        e0, e1 = center[0, :, here].astype(jnp.float32), center[1, :, here].astype(jnp.float32)
        for d in range(dates):
            s0 = sec[d, 0:rows, here].astype(jnp.float32)
            s1 = sec[d, rows:, here].astype(jnp.float32)
            prod[3 * d * rows : (3 * d + 1) * rows, here] = (e0 * s0 + e1 * s1).astype(jnp.bfloat16)
            prod[(3 * d + 1) * rows : (3 * d + 2) * rows, here] = (e1 * s0 - e0 * s1).astype(jnp.bfloat16)
        prod[3 * dates * rows :, here] = (e0 * e0 + e1 * e1).astype(jnp.bfloat16)
        return 0

    lax.fori_loop(0, n_blocks, cross_block, 0)

    box_load.wait()
    high, low = two_terms(dot(prod[...], boxes[...]))
    looks[...] = dot(row_box[...], high) + dot(row_box[...], low)
    n_own = kinds * look_rows
    edge_out[0] = looks[n_own : n_own + 8 * kinds, :]
    edge_out[1] = looks[n_own + 8 * kinds :, :]

    def edge_copy(side):
        return pltpu.make_async_remote_copy(
            src_ref=edge_out.at[side],
            dst_ref=edge_in.at[1 - side],
            send_sem=e_send.at[side],
            recv_sem=e_recv.at[1 - side],
            device_id=(me, up if side == 0 else down),
            device_id_type=MESH,
        )

    @pl.when(has_up)
    def _():
        edge_copy(0).start()

    @pl.when(has_down)
    def _():
        edge_copy(1).start()

    @pl.when(has_up)
    def _():
        edge_copy(1).wait_recv()

    @pl.when(has_down)
    def _():
        edge_copy(0).wait_recv()

    def summed(kind):
        here = looks[kind * look_rows : (kind + 1) * look_rows, :]
        above = edge_in[0, 8 * kind : 8 * kind + 8, :]
        below = edge_in[1, 8 * kind : 8 * kind + 8, :]
        parts = [here[0:8] + above, here[look_rows - 8 :] + below]
        if look_rows > 16:
            parts.insert(1, here[8 : look_rows - 8])
        return jnp.concatenate(parts, axis=0)

    reference_power = summed(3 * dates)
    parts = [[], []]
    for d in range(dates):
        scale = 1.0 / jnp.sqrt(reference_power * summed(3 * d + 2) + EPS)
        for c in range(2):
            parts[c].append(summed(3 * d + c) * scale)
    gamma = jnp.concatenate(parts[0] + parts[1], axis=0)
    gamma = gamma.astype(jnp.bfloat16)
    for j in range(n):
        strip_out[j] = gamma[:, j * strip : (j + 1) * strip]

    def strip_copy(to, slot):
        return pltpu.make_async_remote_copy(
            src_ref=strip_out.at[to],
            dst_ref=strip_in.at[slot],
            send_sem=s_send.at[to],
            recv_sem=s_recv.at[slot],
            device_id=(to, az),
            device_id_type=MESH,
        )

    def send_strip(s, _):
        strip_copy((me + s) % n, me).start()
        return 0

    lax.fori_loop(1, n, send_strip, 0)
    strip_in[me] = strip_out[me]

    @pl.when(has_up)
    def _():
        rim_copy(0).wait_send()
        edge_copy(0).wait_send()

    @pl.when(has_down)
    def _():
        rim_copy(1).wait_send()
        edge_copy(1).wait_send()

    for way, last in ((0, chips - 1), (1, 1)):

        @pl.when(pos != last)
        def _():
            for i in range(n_pieces):
                ring_copy(i, way, core, center).wait_send()

        @pl.when(pos > 0)
        def _():
            for i in range(n_pieces):
                core_copy(i, way, core, center).wait_send()

    @pl.when(is_source)
    def _():
        for i in range(n_pieces):
            for way in range(2):
                for stream in range(2):
                    core_copy(i, way, stream, center).wait_send()

    def hear_strip(s, _):
        other = (me + s) % n
        strip_copy(other, other).wait_recv()
        strip_copy(other, other).wait_send()
        return 0

    lax.fori_loop(1, n, hear_strip, 0)

    half = dates * look_rows
    coh_ref[...] = strip_in[...]

    def magnitude(j, total):
        v = strip_in[j].astype(jnp.float32)
        sq = v * v
        return total + jnp.sqrt(sq[0:half] + sq[half : 2 * half])

    total = lax.fori_loop(0, n, magnitude, jnp.zeros((half, strip), jnp.float32))
    mean = total[0:look_rows]
    for d in range(1, dates):
        mean = mean + total[d * look_rows : (d + 1) * look_rows]
    mean_ref[...] = mean * (1.0 / (n * dates))


def body(n, n_az, slc, az_shift, rg_shift, az_frac, rg_frac):
    dates, _, rows, cols = slc.shape
    kinds = 3 * dates + 1
    look_rows, look_cols = rows // LOOK_AZ, cols // LOOK_RG
    lanes = -(-look_cols // LANE) * LANE
    strip = look_cols // n
    tall = 2 * dates * look_rows
    bf, f32 = jnp.bfloat16, jnp.float32
    smem = pl.BlockSpec(memory_space=pltpu.SMEM)
    vmem = pl.BlockSpec(memory_space=pltpu.VMEM)
    anym = pl.BlockSpec(memory_space=pl.ANY)
    dma = pltpu.SemaphoreType.DMA
    strips, mean = pl.pallas_call(
        functools.partial(kernel, n, n_az, dates, rows, cols),
        out_shape=(
            jax.ShapeDtypeStruct((n, tall, strip), bf),
            jax.ShapeDtypeStruct((look_rows, strip), f32),
        ),
        in_specs=[smem] * 5 + [anym, anym, vmem],
        out_specs=(vmem, vmem),
        scratch_shapes=[
            pltpu.VMEM((dates, 2 * rows, cols + 2 * LANE), bf),
            pltpu.VMEM((2, dates, 2 * RIM, cols), bf),
            pltpu.VMEM((2, dates, 2 * RIM, cols + 2 * LANE), bf),
            pltpu.VMEM((2, rows, cols), bf),
            pltpu.VMEM((cols, lanes), bf),
            pltpu.VMEM((dates, 2, 2 * BLOCK, BLOCK), bf),
            pltpu.VMEM((dates, 4 * rows, 2 * rows + 4 * RIM), bf),
            pltpu.VMEM((dates, 2 * rows + 4 * RIM, cols), bf),
            pltpu.VMEM((dates, 2 * rows, cols), bf),
            pltpu.VMEM((kinds * rows, cols), bf),
            pltpu.VMEM((kinds * (look_rows + 16), lanes), f32),
            pltpu.VMEM((2, 8 * kinds, lanes), f32),
            pltpu.VMEM((2, 8 * kinds, lanes), f32),
            pltpu.VMEM((n, tall, strip), bf),
            pltpu.VMEM((n, tall, strip), bf),
            dma((dates, 2)),
            dma,
            dma,
            dma((2,)),
            dma((2,)),
            dma((2, PIECES)),
            dma((2, 2, PIECES)),
            dma((2, 2, PIECES)),
            dma((2,)),
            dma((2,)),
            dma((n,)),
            dma((n,)),
        ],
        compiler_params=pltpu.CompilerParams(
            collective_id=0, has_side_effects=True, vmem_limit_bytes=60 * 1024 * 1024
        ),
    )(
        az_shift, rg_shift, az_frac, rg_frac, jnp.asarray(kernel_bank()), slc,
        column_boxes(cols, lanes), row_boxes(kinds, rows),
    )
    strips = strips.reshape(n, 2, dates, look_rows, strip)
    coherence = jnp.transpose(strips, (4, 3, 1, 0, 2)).reshape(strip, look_rows, 2, n * dates)
    return coherence, mean.T


def solution(mesh):
    placed = (P("date", None, "az", None), P("date"), P("date"), P("date"), P("date"))
    return jax.shard_map(
        functools.partial(body, mesh.shape["date"], mesh.shape["az"]),
        mesh=mesh,
        in_specs=placed,
        out_specs=(P("date", "az", None, None), P("date", "az")),
        check_vma=False,
    )
```

```python
import functools

import jax
import jax.numpy as jnp
import numpy as np
from jax import lax
from jax.experimental import pallas as pl
from jax.experimental.pallas import tpu as pltpu
from jax.sharding import PartitionSpec as P

TAPS = 8
KBANK = 16
MAXOFF = 4
LOOK_AZ = 4
LOOK_RG = 16
WINDOW = 7
EPS = 1e-06

LEFT = TAPS // 2 - 1
RADIUS = WINDOW // 2
RIM = MAXOFF + TAPS // 2
LANE = 128
BLOCK = 2 * LANE
CHUNK = 16
PIECES = 4
MESH = pl.DeviceIdType.MESH


def kernel_bank():
    fraction = np.arange(KBANK, dtype=np.float64)[:, None] / KBANK
    offset = np.arange(TAPS, dtype=np.float64)[None, :] - LEFT - fraction
    shaped = np.sinc(offset) * (0.5 + 0.5 * np.cos(np.pi * offset / (TAPS // 2 + 0.5)))
    return (shaped / shaped.sum(axis=1, keepdims=True)).astype(np.float32)


def column_boxes(cols, lanes):
    look = np.arange(cols)[:, None] // LOOK_RG
    place = np.arange(lanes)[None, :]
    inside = (np.abs(look - place) <= RADIUS) & (place < cols // LOOK_RG)
    return jnp.asarray(inside, jnp.bfloat16)


def row_boxes(kinds, rows):
    looks = rows // LOOK_AZ
    kind_in = np.arange(kinds * rows) // rows
    look_in = (np.arange(kinds * rows) % rows) // LOOK_AZ
    kind_out = np.concatenate([np.repeat(np.arange(kinds), looks)] + [np.repeat(np.arange(kinds), 8)] * 2)
    look_out = np.concatenate(
        [
            np.tile(np.arange(looks), kinds),
            np.tile(np.arange(8) - 8, kinds),
            np.tile(np.arange(8) + looks, kinds),
        ]
    )
    inside = (kind_in[None] == kind_out[:, None]) & (np.abs(look_in[None] - look_out[:, None]) <= RADIUS)
    return jnp.asarray(inside / (LOOK_AZ * LOOK_RG), jnp.bfloat16)


def two_terms(x):
    high = x.astype(jnp.bfloat16)
    return high, (x - high.astype(jnp.float32)).astype(jnp.bfloat16)


def banded(tap, weights):
    out = jnp.zeros(tap.shape, jnp.float32)
    for j in range(TAPS):
        out = jnp.where(tap == j, weights[j], out)
    return out


def dot(a, b):
    return jnp.dot(a, b, preferred_element_type=jnp.float32)


def kernel(
    n, n_az, dates, rows, cols,
    az_shift, rg_shift, az_frac, rg_frac, bank, slc, boxes_hbm, row_box,
    coh_ref, mean_ref,
    own, rim_out, rim_in, center, boxes, toep, azm, ranged, sec, prod, looks, edge_out, edge_in,
    strip_out, strip_in,
    load_sem, box_sem, own_sem, rim_send, rim_recv, c_ring, c_core, c_recv, e_send, e_recv, s_send, s_recv,
):
    me, az = lax.axis_index("date"), lax.axis_index("az")
    chips = n // 2
    chip, core = me // 2, me % 2
    n_pieces = c_recv.shape[2]
    piece = 2 * cols // n_pieces

    def snake(p):
        return (p // 2) * 2 + (p + p // 2) % 2

    pos = snake(chip)
    onward = snake((pos + 1) % chips) * 2
    back = snake((pos + chips - 1) % chips) * 2
    up, down = jnp.maximum(az - 1, 0), jnp.minimum(az + 1, n_az - 1)
    has_up, has_down = az > 0, az < n_az - 1

    kinds = 3 * dates + 1
    look_rows = rows // LOOK_AZ
    strip = cols // LOOK_RG // n
    n_blocks = cols // BLOCK
    inner = pl.ds(LANE, cols)

    loads = [
        pltpu.make_async_copy(slc.at[d, c], own.at[d, pl.ds(c * rows, rows), inner], load_sem.at[d, c])
        for d in range(dates)
        for c in range(2)
    ]
    for load in loads:
        load.start()
    box_load = pltpu.make_async_copy(boxes_hbm, boxes, box_sem)
    box_load.start()

    barrier = pltpu.get_barrier_semaphore()

    def greet(s, _):
        pl.semaphore_signal(barrier, inc=1, device_id=((me + s) % n, az), device_id_type=MESH)
        return 0

    lax.fori_loop(1, n, greet, 0)

    @pl.when(has_up)
    def _():
        pl.semaphore_signal(barrier, inc=1, device_id=(me, up), device_id_type=MESH)

    @pl.when(has_down)
    def _():
        pl.semaphore_signal(barrier, inc=1, device_id=(me, down), device_id_type=MESH)

    for d in range(dates):
        for lo in (0, LANE + cols):
            own[d, :, lo : lo + LANE] = jnp.zeros((2 * rows, LANE), jnp.bfloat16)
            for side in range(2):
                rim_in[side, d, :, lo : lo + LANE] = jnp.zeros((2 * RIM, LANE), jnp.bfloat16)

    @pl.when(jnp.logical_not(has_up))
    def _():
        rim_in[0, :, :, LANE : LANE + cols] = jnp.zeros((dates, 2 * RIM, cols), jnp.bfloat16)
        edge_in[0] = jnp.zeros(edge_in.shape[1:], jnp.float32)

    @pl.when(jnp.logical_not(has_down))
    def _():
        rim_in[1, :, :, LANE : LANE + cols] = jnp.zeros((dates, 2 * RIM, cols), jnp.bfloat16)
        edge_in[1] = jnp.zeros(edge_in.shape[1:], jnp.float32)

    n_here = has_up.astype(jnp.int32) + has_down.astype(jnp.int32)
    pl.semaphore_wait(barrier, n - 1 + n_here)

    def rim_copy(side):
        return pltpu.make_async_remote_copy(
            src_ref=rim_out.at[side],
            dst_ref=rim_in.at[1 - side, :, :, inner],
            send_sem=rim_send.at[side],
            recv_sem=rim_recv.at[1 - side],
            device_id=(me, up if side == 0 else down),
            device_id_type=MESH,
        )

    def place(i, way, stream):
        r = pl.multiple_of(way * (rows // 2) + stream * (rows // 4), CHUNK)
        c = pl.multiple_of((i // 2) * piece, LANE)
        return i % 2, pl.ds(r, rows // 4), pl.ds(c, piece)

    def chunk_copy(i, way, stream, source, to, send_sem):
        where = place(i, way, stream)
        return pltpu.make_async_remote_copy(
            src_ref=source.at[where],
            dst_ref=center.at[where],
            send_sem=send_sem,
            recv_sem=c_recv.at[way, stream, i],
            device_id=(to, az),
            device_id_type=MESH,
        )

    def ring_copy(i, way, stream, source):
        return chunk_copy(i, way, stream, source, (onward if way == 0 else back) + stream, c_ring.at[way, stream, i])

    def core_copy(i, way, stream, source):
        return chunk_copy(i, way, stream, source, sibling, c_core.at[way, stream, i])

    is_source = jnp.logical_and(pos == 0, core == 0)
    sibling = chip * 2 + (1 - core)
    own_center = pltpu.make_async_copy(slc.at[0], center, own_sem)

    @pl.when(is_source)
    def _():
        for i in range(n_pieces):
            for way in range(2):
                for stream in range(2):
                    ring_copy(i, way, stream, slc.at[0]).start()
        for i in range(n_pieces):
            for way in range(2):
                for stream in range(2):
                    core_copy(i, way, stream, slc.at[0]).start()
        own_center.start()

    for load in loads:
        load.wait()

    for d in range(dates):
        for side, lo in ((0, 0), (1, rows - 16)):
            cut = slice(0, RIM) if side == 0 else slice(16 - RIM, 16)
            both = [
                own[d, c * rows + lo : c * rows + lo + 16, LANE : LANE + cols].astype(jnp.float32)[cut]
                for c in range(2)
            ]
            rim_out[side, d] = jnp.concatenate(both, axis=0).astype(jnp.bfloat16)

    @pl.when(has_up)
    def _():
        rim_copy(0).start()

    @pl.when(has_down)
    def _():
        rim_copy(1).start()

    def relay_step(t):
        for way, hops, last in ((0, pos, chips - 1), (1, chips - pos, 1)):
            i = t - hops

            @pl.when((pos > 0) & (i >= 0) & (i < n_pieces))
            def _():
                ring_copy(i, way, core, center).wait_recv()

                @pl.when(pos != last)
                def _():
                    ring_copy(i, way, core, center).start()

                core_copy(i, way, core, center).start()

    steps = [functools.partial(relay_step, t) for t in range(1, chips + n_pieces - 1)]

    for d in range(dates):
        weights = [bank[rg_frac[d], j] for j in range(TAPS)]
        across = lax.broadcasted_iota(jnp.int32, (LANE, LANE), 0) - lax.broadcasted_iota(jnp.int32, (LANE, LANE), 1)
        for b in range(3):
            terms = two_terms(banded(across + (LANE * (b - 1) + LEFT - rg_shift[d]), weights))
            for k in range(2):
                for right in range(2):
                    toep[d, k, LANE * (b + right) : LANE * (b + right + 1), LANE * right : LANE * (right + 1)] = terms[k]
        for k in range(2):
            zero = jnp.zeros((LANE, LANE), jnp.bfloat16)
            toep[d, k, 0:LANE, LANE:] = zero
            toep[d, k, 3 * LANE :, 0:LANE] = zero

    deep = 2 * rows + 4 * RIM
    for d in range(dates):
        weights = [bank[az_frac[d], j] for j in range(TAPS)]
        out = lax.broadcasted_iota(jnp.int32, (2 * rows, deep), 0)
        src = lax.broadcasted_iota(jnp.int32, (2 * rows, deep), 1)
        rim = src - 2 * rows
        in_own = rim < 0
        rim = jnp.maximum(rim, 0)
        rim_row = lax.rem(rim, RIM)
        src_part = jnp.where(in_own, lax.div(src, rows), lax.rem(lax.div(rim, RIM), 2))
        src_row = jnp.where(in_own, lax.rem(src, rows), jnp.where(rim < 2 * RIM, rim_row - RIM, rim_row + rows))
        tap = src_row - lax.rem(out, rows) + (LEFT - az_shift[d])
        tap = jnp.where(src_part == lax.div(out, rows), tap, -1)
        terms = two_terms(banded(tap, weights))
        for k in range(2):
            azm[d, k * 2 * rows : (k + 1) * 2 * rows, :] = terms[k]

    def range_block(k, _):
        window = pl.ds(pl.multiple_of(k * BLOCK, LANE), 2 * BLOCK)
        here = pl.ds(pl.multiple_of(k * BLOCK, LANE), BLOCK)
        for d in range(dates):
            x = own[d, :, window]
            ranged[d, 0 : 2 * rows, here] = (dot(x, toep[d, 0]) + dot(x, toep[d, 1])).astype(jnp.bfloat16)
        return 0

    def range_rims(_):
        @pl.when(has_up)
        def _():
            rim_copy(1).wait_recv()

        @pl.when(has_down)
        def _():
            rim_copy(0).wait_recv()

        for d in range(dates):
            x = jnp.concatenate(
                [rim_in[side, d, :, k * BLOCK : (k + 2) * BLOCK] for k in range(n_blocks) for side in range(2)], axis=0
            )
            y = (dot(x, toep[d, 0]) + dot(x, toep[d, 1])).astype(jnp.bfloat16)
            for k in range(n_blocks):
                ranged[d, 2 * rows :, k * BLOCK : (k + 1) * BLOCK] = y[4 * RIM * k : 4 * RIM * (k + 1)]

    def az_block(k, _):
        here = pl.ds(pl.multiple_of(k * BLOCK, LANE), BLOCK)
        for d in range(dates):
            both = dot(azm[d], ranged[d, :, here])
            s = both[0 : 2 * rows] + both[2 * rows :]
            sec[d, :, here] = s.astype(jnp.bfloat16)
            power = s[0:rows] * s[0:rows] + s[rows:] * s[rows:]
            prod[(3 * d + 2) * rows : (3 * d + 3) * rows, here] = power.astype(jnp.bfloat16)
        return 0

    third = n_blocks // 3
    work = [functools.partial(lax.fori_loop, k * third, (k + 1) * third, range_block) for k in range(3)]
    work += [range_rims]
    work += [functools.partial(lax.fori_loop, k * third, (k + 1) * third, az_block) for k in range(3)]
    for k in range(max(len(steps), len(work))):
        if k < len(work):
            work[k](0)
        if k < len(steps):
            steps[k]()

    @pl.when(is_source)
    def _():
        own_center.wait()

    @pl.when(jnp.logical_not(is_source))
    def _():
        for i in range(n_pieces):
            for way in range(2):
                core_copy(i, way, 1 - core, center).wait_recv()

    @pl.when((pos == 0) & (core != 0))
    def _():
        for i in range(n_pieces):
            for way in range(2):
                core_copy(i, way, core, center).wait_recv()

    def cross_block(k, _):
        here = pl.ds(pl.multiple_of(k * BLOCK, LANE), BLOCK)
        e0, e1 = center[0, :, here].astype(jnp.float32), center[1, :, here].astype(jnp.float32)
        for d in range(dates):
            s0 = sec[d, 0:rows, here].astype(jnp.float32)
            s1 = sec[d, rows:, here].astype(jnp.float32)
            prod[3 * d * rows : (3 * d + 1) * rows, here] = (e0 * s0 + e1 * s1).astype(jnp.bfloat16)
            prod[(3 * d + 1) * rows : (3 * d + 2) * rows, here] = (e1 * s0 - e0 * s1).astype(jnp.bfloat16)
        prod[3 * dates * rows :, here] = (e0 * e0 + e1 * e1).astype(jnp.bfloat16)
        return 0

    lax.fori_loop(0, n_blocks, cross_block, 0)

    box_load.wait()
    high, low = two_terms(dot(prod[...], boxes[...]))
    looks[...] = dot(row_box[...], high) + dot(row_box[...], low)
    n_own = kinds * look_rows
    edge_out[0] = looks[n_own : n_own + 8 * kinds, :]
    edge_out[1] = looks[n_own + 8 * kinds :, :]

    def edge_copy(side):
        return pltpu.make_async_remote_copy(
            src_ref=edge_out.at[side],
            dst_ref=edge_in.at[1 - side],
            send_sem=e_send.at[side],
            recv_sem=e_recv.at[1 - side],
            device_id=(me, up if side == 0 else down),
            device_id_type=MESH,
        )

    @pl.when(has_up)
    def _():
        edge_copy(0).start()

    @pl.when(has_down)
    def _():
        edge_copy(1).start()

    @pl.when(has_up)
    def _():
        edge_copy(1).wait_recv()

    @pl.when(has_down)
    def _():
        edge_copy(0).wait_recv()

    def summed(kind):
        here = looks[kind * look_rows : (kind + 1) * look_rows, :]
        above = edge_in[0, 8 * kind : 8 * kind + 8, :]
        below = edge_in[1, 8 * kind : 8 * kind + 8, :]
        parts = [here[0:8] + above, here[look_rows - 8 :] + below]
        if look_rows > 16:
            parts.insert(1, here[8 : look_rows - 8])
        return jnp.concatenate(parts, axis=0)

    reference_power = summed(3 * dates)
    parts = [[], []]
    for d in range(dates):
        scale = 1.0 / jnp.sqrt(reference_power * summed(3 * d + 2) + EPS)
        for c in range(2):
            parts[c].append(summed(3 * d + c) * scale)
    gamma = jnp.concatenate(parts[0] + parts[1], axis=0)
    gamma = gamma.astype(jnp.bfloat16)
    for j in range(n):
        strip_out[j] = gamma[:, j * strip : (j + 1) * strip]

    def strip_copy(to, slot):
        return pltpu.make_async_remote_copy(
            src_ref=strip_out.at[to],
            dst_ref=strip_in.at[slot],
            send_sem=s_send.at[to],
            recv_sem=s_recv.at[slot],
            device_id=(to, az),
            device_id_type=MESH,
        )

    def send_strip(s, _):
        strip_copy((me + s) % n, me).start()
        return 0

    lax.fori_loop(1, n, send_strip, 0)
    strip_in[me] = strip_out[me]

    @pl.when(has_up)
    def _():
        rim_copy(0).wait_send()
        edge_copy(0).wait_send()

    @pl.when(has_down)
    def _():
        rim_copy(1).wait_send()
        edge_copy(1).wait_send()

    for way, last in ((0, chips - 1), (1, 1)):

        @pl.when((pos > 0) & (pos != last))
        def _():
            for i in range(n_pieces):
                ring_copy(i, way, core, center).wait_send()

        @pl.when(pos > 0)
        def _():
            for i in range(n_pieces):
                core_copy(i, way, core, center).wait_send()

    @pl.when(is_source)
    def _():
        for i in range(n_pieces):
            for way in range(2):
                for stream in range(2):
                    ring_copy(i, way, stream, center).wait_send()
                    core_copy(i, way, stream, center).wait_send()

    def hear_strip(s, _):
        other = (me + s) % n
        strip_copy(other, other).wait_recv()
        strip_copy(other, other).wait_send()
        return 0

    lax.fori_loop(1, n, hear_strip, 0)

    half = dates * look_rows
    coh_ref[...] = strip_in[...]

    def magnitude(j, total):
        v = strip_in[j].astype(jnp.float32)
        sq = v * v
        return total + jnp.sqrt(sq[0:half] + sq[half : 2 * half])

    total = lax.fori_loop(0, n, magnitude, jnp.zeros((half, strip), jnp.float32))
    mean = total[0:look_rows]
    for d in range(1, dates):
        mean = mean + total[d * look_rows : (d + 1) * look_rows]
    mean_ref[...] = mean * (1.0 / (n * dates))


def body(n, n_az, slc, az_shift, rg_shift, az_frac, rg_frac):
    dates, _, rows, cols = slc.shape
    kinds = 3 * dates + 1
    look_rows, look_cols = rows // LOOK_AZ, cols // LOOK_RG
    lanes = -(-look_cols // LANE) * LANE
    strip = look_cols // n
    tall = 2 * dates * look_rows
    bf, f32 = jnp.bfloat16, jnp.float32
    smem = pl.BlockSpec(memory_space=pltpu.SMEM)
    vmem = pl.BlockSpec(memory_space=pltpu.VMEM)
    anym = pl.BlockSpec(memory_space=pl.ANY)
    dma = pltpu.SemaphoreType.DMA
    strips, mean = pl.pallas_call(
        functools.partial(kernel, n, n_az, dates, rows, cols),
        out_shape=(
            jax.ShapeDtypeStruct((n, tall, strip), bf),
            jax.ShapeDtypeStruct((look_rows, strip), f32),
        ),
        in_specs=[smem] * 5 + [anym, anym, vmem],
        out_specs=(vmem, vmem),
        scratch_shapes=[
            pltpu.VMEM((dates, 2 * rows, cols + 2 * LANE), bf),
            pltpu.VMEM((2, dates, 2 * RIM, cols), bf),
            pltpu.VMEM((2, dates, 2 * RIM, cols + 2 * LANE), bf),
            pltpu.VMEM((2, rows, cols), bf),
            pltpu.VMEM((cols, lanes), bf),
            pltpu.VMEM((dates, 2, 2 * BLOCK, BLOCK), bf),
            pltpu.VMEM((dates, 4 * rows, 2 * rows + 4 * RIM), bf),
            pltpu.VMEM((dates, 2 * rows + 4 * RIM, cols), bf),
            pltpu.VMEM((dates, 2 * rows, cols), bf),
            pltpu.VMEM((kinds * rows, cols), bf),
            pltpu.VMEM((kinds * (look_rows + 16), lanes), f32),
            pltpu.VMEM((2, 8 * kinds, lanes), f32),
            pltpu.VMEM((2, 8 * kinds, lanes), f32),
            pltpu.VMEM((n, tall, strip), bf),
            pltpu.VMEM((n, tall, strip), bf),
            dma((dates, 2)),
            dma,
            dma,
            dma((2,)),
            dma((2,)),
            dma((2, 2, PIECES)),
            dma((2, 2, PIECES)),
            dma((2, 2, PIECES)),
            dma((2,)),
            dma((2,)),
            dma((n,)),
            dma((n,)),
        ],
        compiler_params=pltpu.CompilerParams(
            collective_id=0, has_side_effects=True, vmem_limit_bytes=60 * 1024 * 1024
        ),
    )(
        az_shift, rg_shift, az_frac, rg_frac, jnp.asarray(kernel_bank()), slc,
        column_boxes(cols, lanes), row_boxes(kinds, rows),
    )
    strips = strips.reshape(n, 2, dates, look_rows, strip)
    coherence = jnp.transpose(strips, (4, 3, 1, 0, 2)).reshape(strip, look_rows, 2, n * dates)
    return coherence, mean.T


def solution(mesh):
    placed = (P("date", None, "az", None), P("date"), P("date"), P("date"), P("date"))
    return jax.shard_map(
        functools.partial(body, mesh.shape["date"], mesh.shape["az"]),
        mesh=mesh,
        in_specs=placed,
        out_specs=(P("date", "az", None, None), P("date", "az")),
        check_vma=False,
    )
```
